32 devices in a mesh: ctx: 16 (over z, y, x), head: 2 (over core).
Axes of the slice: x: 2, y: 2, z: 4, core: 2. Of those that a mesh axis runs over, the one named last changes fastest.
Arguments:
- queries: bfloat16 [4096, 4096], P('ctx', 'head'), may hold values from -6.5 to 6.5
- keyval: bfloat16 [2, 4096, 1024], P(None, 'ctx', 'head'), may hold values from -6 to 6
- out_gain: float32 [4096], P('head'), may hold values from 0.1 to 1.9
Outputs:
- attended: bfloat16 [4096, 4096], P('ctx', 'head')
The draws below stay inside these ranges and needn't reach their ends.
All inputs are finite; a program needn't handle non-finite values.
Results may differ from the reference program's by a relative error of at most 0.0049.
Values may be sent and summed in bfloat16 or wider, within the bound.
A program may use at most 64 MiB of HBM per device.

```python
import jax
import jax.numpy as jnp
from jax import lax

HEADS = 32
KV_HEADS = 8
HD = 128
BLK = 128
TOKENS = 4096


def draw_queries(key, part):
    group_size = HEADS // KV_HEADS
    result = jnp.clip(jax.random.normal(jax.random.fold_in(key, 21), (TOKENS, KV_HEADS, group_size, HD), jnp.float32), -6.0, 6.0)
    return result.reshape(TOKENS, HEADS * HD).astype(jnp.bfloat16)


def draw_keyval(key, part):
    value_part = jnp.clip(jax.random.normal(jax.random.fold_in(key, 32), (TOKENS, KV_HEADS * HD), jnp.float32), -6.0, 6.0)
    key_part = jnp.clip(jax.random.normal(jax.random.fold_in(key, 31), (TOKENS, KV_HEADS, HD), jnp.float32), -6.0, 6.0)
    return jnp.stack([key_part.reshape(TOKENS, KV_HEADS * HD), value_part]).astype(jnp.bfloat16)


def setup_inputs(seed: int = 0) -> dict:
    streams_of = jax.random.split(jax.random.key(seed), 4)
    return {
        "queries": draw_queries(jax.random.fold_in(streams_of[3], 71), 0),
        "keyval": draw_keyval(jax.random.fold_in(streams_of[3], 71), 0),
        "out_gain": jnp.clip(1.0 + 0.18 * jax.random.normal(streams_of[2], (HEADS * HD,), jnp.float32), 0.1, 1.9),
    }


def reference(queries, keyval, out_gain):
    tok_total = queries.shape[0]
    nblocks = tok_total // BLK
    group_size = HEADS // KV_HEADS
    gap_list = jnp.array([0] + [2 ** power_exp for power_exp in range(nblocks.bit_length() - 1)], jnp.int32)
    q_blocks = queries.reshape(nblocks, BLK, KV_HEADS, group_size, HD)
    kv_blocks = keyval.reshape(2, nblocks, BLK, KV_HEADS, HD)
    lower_tri = jnp.arange(BLK)[:, None] >= jnp.arange(BLK)[None, :]
    own_slot = jnp.arange(gap_list.shape[0]) == 0
    score_scale = HD ** (-0.5)

    def one_block(block_id):
        sources = block_id - gap_list
        valid_slot = sources >= 0
        picks = jnp.maximum(sources, 0).astype(jnp.int32)
        key_rows = kv_blocks[0][picks]
        value_rows = kv_blocks[1][picks]
        query_rows = lax.dynamic_index_in_dim(q_blocks, block_id, 0, keepdims=False)
        scores = jnp.einsum('qhgd,skhd->hgqsk', query_rows.astype(jnp.float32), key_rows.astype(jnp.float32)) * score_scale
        allowed = valid_slot[None, :, None] & (own_slot[None, :, None] | lower_tri[:, None, :])
        scores = jnp.where(allowed[None, None], scores, -jnp.inf)
        row_max = lax.optimization_barrier(jnp.max(scores, axis=(3, 4), keepdims=True))
        weights = jnp.exp(scores - row_max)
        row_sum = lax.optimization_barrier(jnp.sum(weights, axis=(3, 4), keepdims=True))
        probabilities = (weights / row_sum).astype(jnp.bfloat16)
        return jnp.einsum('hgqsk,skhd->qhgd', probabilities.astype(jnp.float32), value_rows.astype(jnp.float32))
    outputs = lax.map(one_block, jnp.arange(nblocks, dtype=jnp.int32))
    combined = outputs.reshape(tok_total, HEADS * HD)
    squares = lax.optimization_barrier(jnp.sum(combined * combined, axis=1))
    inverse = lax.rsqrt(squares / (HEADS * HD) + 1e-06)
    return (combined * inverse[:, None] * out_gain[None, :]).astype(jnp.bfloat16)
```

```python
import functools
import math

import jax
import jax.numpy as jnp
from jax import lax
from jax.experimental import pallas as pl
from jax.experimental.pallas import tpu as pltpu
from jax.sharding import PartitionSpec as P

HD = 128
BLK = 128
MESH = pl.DeviceIdType.MESH
F32 = jnp.float32
BF16 = jnp.bfloat16


def kernel(
    ctx, levels, kvh, group, features,
    q_hbm, kv_hbm, gain_ref, out_ref,
    kvbuf, qbuf, acc, mbuf, ssq, ssq_peer,
    qsem, kvsem, send_sem, recv_sem, nsend, nrecv,
):
    p = lax.axis_index("ctx")
    core = lax.axis_index("head")
    c = HD ** (-0.5) * math.log2(math.e)
    rows = group * BLK
    bit0 = lax.rem(p, 2)
    bit1 = lax.rem(p // 2, 2)

    def kv_load(h):
        return pltpu.make_async_copy(
            kv_hbm.at[:, :, pl.ds(h * HD, HD)], kvbuf.at[0, h], kvsem.at[h]
        )

    def q_load(h):
        return pltpu.make_async_copy(
            q_hbm.at[:, pl.ds(h * HD, HD)], qbuf.at[h], qsem.at[h]
        )

    for h in range(kvh):
        kv_load(h).start()
    for h in range(kvh * group):
        q_load(h).start()

    barrier = pltpu.get_barrier_semaphore()
    shifts = [1, 2, 4] + [2**k for k in range(4, levels)]
    expect = jnp.int32(1)
    pl.semaphore_signal(barrier, inc=1, device_id={"head": 1 - core}, device_id_type=MESH)
    for s in shifts:
        up = p + s < ctx
        down = p >= s

        @pl.when(up)
        def _():
            pl.semaphore_signal(barrier, inc=1, device_id={"ctx": p + s}, device_id_type=MESH)

        @pl.when(down)
        def _():
            pl.semaphore_signal(barrier, inc=1, device_id={"ctx": p - s}, device_id_type=MESH)

        expect = expect + up.astype(jnp.int32) + down.astype(jnp.int32)
    pl.semaphore_wait(barrier, expect)

    def send(src, dst, kind, h, target):
        return pltpu.make_async_remote_copy(
            src_ref=kvbuf.at[src, h],
            dst_ref=kvbuf.at[dst, h],
            send_sem=send_sem.at[kind, h],
            recv_sem=recv_sem.at[dst - 1, h],
            device_id={"ctx": target},
            device_id_type=MESH,
        )

    own_sends = [
        (p + 4 < ctx, 0, 3, 2, p + 4),
        (bit1 == 0, 0, 2, 1, p + 2),
        (bit0 == 0, 0, 1, 0, p + 1),
    ] + [(p + 2**k < ctx, 0, k + 1, k + 2, p + 2**k) for k in range(4, levels)]
    from_l2 = [
        (jnp.logical_and(p >= 4, p + 4 < ctx), 3, 4, 4, p + 4),
        (jnp.logical_and(p >= 4, bit1 == 1), 3, 2, 3, p - 2),
    ]
    from_l1 = [(jnp.logical_and(p >= 2, bit0 == 1), 2, 1, 5, p - 1)]

    def start(plan, h):
        for cond, src, dst, kind, target in plan:

            @pl.when(cond)
            def _():
                send(src, dst, kind, h, target).start()

    def arrived(level, h):
        send(0, level + 1, 0, h, p + 1 - 2 * bit0).wait_recv()

    for h in range(kvh):
        kv_load(h).wait()
        start(own_sends, h)

    ones = jnp.ones((2 * BLK, HD), BF16)
    lower = (
        lax.broadcasted_iota(jnp.int32, (group, BLK, BLK), 1)
        >= lax.broadcasted_iota(jnp.int32, (group, BLK, BLK), 2)
    ).reshape(rows, BLK)

    def step(h, b, slot, lo, nk, first=False, full=-1):
        idx = h * 2 + b
        q = qbuf[pl.ds(h * group, group), b * BLK : (b + 1) * BLK, :].reshape(rows, HD)
        k = kvbuf[slot, h, 0, lo : lo + nk, :]
        v = kvbuf[slot, h, 1, lo : lo + nk, :]
        s = lax.dot_general(q, k, (((1,), (1,)), ((), ())), preferred_element_type=F32)
        parts = [s[:, i : i + BLK] for i in range(0, nk, BLK)]
        parts = [x if i == full else jnp.where(lower, x, -jnp.inf) for i, x in enumerate(parts)]
        top = functools.reduce(jnp.maximum, parts)
        top = jnp.broadcast_to(jnp.max(top, axis=1, keepdims=True), (rows, BLK))
        if not first:
            old = mbuf[idx]
            top = jnp.maximum(old, top)
        w = jnp.concatenate([jnp.exp2((x - top) * c).astype(BF16) for x in parts], axis=1)
        pv = jnp.dot(
            w, jnp.concatenate([v, ones[:nk]], axis=1), preferred_element_type=F32
        )
        mbuf[idx] = top
        if first:
            acc[idx] = pv
        else:
            alpha = jnp.exp2((old - top) * c)
            acc[idx] = acc[idx] * jnp.concatenate([alpha, alpha], axis=1) + pv

    for h in range(kvh * group):
        q_load(h).wait()

    @pl.loop(0, kvh)
    def _(h):
        step(h, 0, 0, 0, BLK, first=True, full=0)
        step(h, 1, 0, 0, 2 * BLK, first=True, full=1)

    @pl.loop(0, kvh + 2)
    def _(i):
        @pl.when(jnp.logical_and(i < kvh, p >= 4))
        def _():
            arrived(2, i)
            start(from_l2, i)

        h1 = jnp.maximum(i - 1, 0)
        on1 = jnp.logical_and(jnp.logical_and(i >= 1, i <= kvh), p >= 2)

        @pl.when(on1)
        def _():
            arrived(1, h1)
            start(from_l1, h1)

        @pl.when(jnp.logical_and(i < kvh, p >= 4))
        def _():
            step(i, 0, 3, 0, BLK)
            step(i, 1, 3, BLK, BLK)

        @pl.when(on1)
        def _():
            step(h1, 0, 2, 0, BLK)
            step(h1, 1, 2, BLK, BLK)

        h0 = jnp.maximum(i - 2, 0)

        @pl.when(jnp.logical_and(i >= 2, p >= 1))
        def _():
            arrived(0, h0)
            step(h0, 0, 1, 0, 2 * BLK)
            step(h0, 1, 1, BLK, BLK)

    ssq[...] = jnp.zeros_like(ssq)

    @pl.loop(0, kvh)
    def _(h):
        for k in range(3, levels):

            @pl.when(p >= 2**k)
            def _():
                arrived(k, h)
                step(h, 0, k + 1, 0, BLK)
                step(h, 1, k + 1, BLK, BLK)

        for b in range(2):
            idx = h * 2 + b
            o = acc[idx, :, :HD] * (1.0 / acc[idx, :, HD:])
            acc[idx, :, :HD] = o
            ssq[b] += jnp.sum((o * o).reshape(group, BLK, HD), axis=0)

    swap = pltpu.make_async_remote_copy(
        src_ref=ssq, dst_ref=ssq_peer, send_sem=nsend, recv_sem=nrecv,
        device_id={"head": 1 - core}, device_id_type=MESH,
    )
    swap.start()

    def drain(plan, h):
        for cond, src, dst, kind, target in plan:

            @pl.when(cond)
            def _():
                send(src, dst, kind, h, target).wait_send()

    for h in range(kvh):
        drain(own_sends + from_l2 + from_l1, h)
    swap.wait()

    for b in range(2):
        total = jnp.sum(ssq[b] + ssq_peer[b], axis=1, keepdims=True)
        inv = jnp.broadcast_to(lax.rsqrt(total / features + 1e-06), (BLK, HD))
        for h in range(kvh):
            for g in range(group):
                cols = slice((h * group + g) * HD, (h * group + g + 1) * HD)
                o = acc[h * 2 + b, g * BLK : (g + 1) * BLK, :HD]
                out_ref[b * BLK : (b + 1) * BLK, cols] = (o * inv * gain_ref[:, cols]).astype(BF16)


def local(queries, keyval, out_gain):
    ctx = lax.axis_size("ctx")
    levels = ctx.bit_length() - 1
    toks = queries.shape[0]
    kvh = keyval.shape[2] // HD
    heads = queries.shape[1] // HD
    group = heads // kvh
    features = queries.shape[1] * lax.axis_size("head")
    kinds = max(6, levels + 2)
    body = functools.partial(kernel, ctx, levels, kvh, group, features)
    return pl.pallas_call(
        body,
        out_shape=jax.ShapeDtypeStruct(queries.shape, BF16),
        in_specs=[
            pl.BlockSpec(memory_space=pltpu.HBM),
            pl.BlockSpec(memory_space=pltpu.HBM),
            pl.BlockSpec(memory_space=pltpu.VMEM),
        ],
        out_specs=pl.BlockSpec(memory_space=pltpu.VMEM),
        scratch_shapes=[
            pltpu.VMEM((levels + 1, kvh, 2, toks, HD), BF16),
            pltpu.VMEM((heads, toks, HD), BF16),
            pltpu.VMEM((kvh * 2, group * BLK, 2 * HD), F32),
            pltpu.VMEM((kvh * 2, group * BLK, HD), F32),
            pltpu.VMEM((2, BLK, HD), F32),
            pltpu.VMEM((2, BLK, HD), F32),
            pltpu.SemaphoreType.DMA((heads,)),
            pltpu.SemaphoreType.DMA((kvh,)),
            pltpu.SemaphoreType.DMA((kinds, kvh)),
            pltpu.SemaphoreType.DMA((levels, kvh)),
            pltpu.SemaphoreType.DMA,
            pltpu.SemaphoreType.DMA,
        ],
        compiler_params=pltpu.CompilerParams(
            collective_id=0, has_side_effects=True, vmem_limit_bytes=40 * 2**20
        ),
        cost_estimate=pl.CostEstimate(
            flops=2 * 2 * 2 * BLK * BLK * HD * heads * (levels + 2),
            bytes_accessed=4 * 2**20,
            transcendentals=2 * BLK * BLK * heads * (levels + 2),
        ),
    )(queries, keyval, out_gain.reshape(1, -1))


def solution(mesh):
    in_specs = (P("ctx", "head"), P(None, "ctx", "head"), P("head"))
    out_specs = P("ctx", "head")
    return jax.shard_map(local, mesh=mesh, in_specs=in_specs, out_specs=out_specs, check_vma=False)
```

```python
import functools
import math

import jax
import jax.numpy as jnp
from jax import lax
from jax.experimental import pallas as pl
from jax.experimental.pallas import tpu as pltpu
from jax.sharding import PartitionSpec as P

HD = 128
BLK = 128
MESH = pl.DeviceIdType.MESH
VMEM_LIMIT = 56 * 2**20
F32 = jnp.float32
BF16 = jnp.bfloat16


def kernel(
    ctx, levels, kvh, group, features,
    q_hbm, kv_hbm, gain_ref, out_hbm,
    kvbuf, qbuf, acc, mbuf, ssq, ssq_peer, obuf,
    qsem, kvsem, send_sem, recv_sem, nsend, nrecv, osem,
):
    p = lax.axis_index("ctx")
    core = lax.axis_index("head")
    c = HD ** (-0.5) * math.log2(math.e)
    rows = group * BLK
    bit0 = lax.rem(p, 2)
    bit1 = lax.rem(p // 2, 2)

    def kv_load(h):
        return pltpu.make_async_copy(
            kv_hbm.at[:, :, pl.ds(h * HD, HD)], kvbuf.at[0, h], kvsem.at[h]
        )

    def q_load(h):
        return pltpu.make_async_copy(
            q_hbm.at[:, pl.ds(h * HD, HD)], qbuf.at[h], qsem.at[h]
        )

    for h in range(kvh):
        kv_load(h).start()
    for h in range(kvh * group):
        q_load(h).start()

    barrier = pltpu.get_barrier_semaphore()
    shifts = [1, 2, 4] + [2**k for k in range(4, levels)]
    expect = jnp.int32(1)
    pl.semaphore_signal(barrier, inc=1, device_id={"head": 1 - core}, device_id_type=MESH)
    for s in shifts:
        up = p + s < ctx
        down = p >= s

        @pl.when(up)
        def _():
            pl.semaphore_signal(barrier, inc=1, device_id={"ctx": p + s}, device_id_type=MESH)

        @pl.when(down)
        def _():
            pl.semaphore_signal(barrier, inc=1, device_id={"ctx": p - s}, device_id_type=MESH)

        expect = expect + up.astype(jnp.int32) + down.astype(jnp.int32)
    pl.semaphore_wait(barrier, expect)

    def send(src, dst, kind, h, target):
        return pltpu.make_async_remote_copy(
            src_ref=kvbuf.at[src, h],
            dst_ref=kvbuf.at[dst, h],
            send_sem=send_sem.at[kind, h],
            recv_sem=recv_sem.at[dst - 1, h],
            device_id={"ctx": target},
            device_id_type=MESH,
        )

    own_sends = [
        (p + 4 < ctx, 0, 3, 2, p + 4),
        (bit1 == 0, 0, 2, 1, p + 2),
        (bit0 == 0, 0, 1, 0, p + 1),
    ] + [(p + 2**k < ctx, 0, k + 1, k + 2, p + 2**k) for k in range(4, levels)]
    onward = [(jnp.logical_and(p >= 4, p + 4 < ctx), 3, 4, 4, p + 4)]
    from_l2 = [(jnp.logical_and(p >= 4, bit1 == 1), 3, 2, 3, p - 2)]
    from_l1 = [(jnp.logical_and(p >= 2, bit0 == 1), 2, 1, 5, p - 1)]

    def start(plan, h):
        for cond, src, dst, kind, target in plan:

            @pl.when(cond)
            def _():
                send(src, dst, kind, h, target).start()

    def arrived(level, h):
        send(0, level + 1, 0, h, p + 1 - 2 * bit0).wait_recv()

    def drain(plan, h):
        for cond, src, dst, kind, target in plan:

            @pl.when(cond)
            def _():
                send(src, dst, kind, h, target).wait_send()

    for h in range(kvh):
        kv_load(h).wait()
        if h < 2:
            start(own_sends, h)

    ones = jnp.ones((2 * BLK, HD), BF16)
    lower = (
        lax.broadcasted_iota(jnp.int32, (group, BLK, BLK), 1)
        >= lax.broadcasted_iota(jnp.int32, (group, BLK, BLK), 2)
    ).reshape(rows, BLK)

    def step(h, b, slot, lo, nk, first=False, full=-1):
        idx = h * 2 + b
        q = qbuf[pl.ds(h * group, group), b * BLK : (b + 1) * BLK, :].reshape(rows, HD)
        k = kvbuf[slot, h, 0, lo : lo + nk, :]
        v = kvbuf[slot, h, 1, lo : lo + nk, :]
        s = lax.dot_general(q, k, (((1,), (1,)), ((), ())), preferred_element_type=F32)
        parts = [s[:, i : i + BLK] for i in range(0, nk, BLK)]
        parts = [x if i == full else jnp.where(lower, x, -jnp.inf) for i, x in enumerate(parts)]
        top = functools.reduce(jnp.maximum, parts)
        top = jnp.broadcast_to(jnp.max(top, axis=1, keepdims=True), (rows, BLK))
        if not first:
            old = mbuf[idx]
            top = jnp.maximum(old, top)
        w = jnp.concatenate([jnp.exp2((x - top) * c).astype(BF16) for x in parts], axis=1)
        pv = jnp.dot(
            w, jnp.concatenate([v, ones[:nk]], axis=1), preferred_element_type=F32
        )
        mbuf[idx] = top
        if first:
            acc[idx] = pv
        else:
            alpha = jnp.exp2((old - top) * c)
            acc[idx] = acc[idx] * jnp.concatenate([alpha, alpha], axis=1) + pv

    for h in range(kvh * group):
        q_load(h).wait()

    @pl.loop(0, kvh)
    def _(h):
        step(h, 0, 0, 0, BLK, first=True, full=0)
        step(h, 1, 0, 0, 2 * BLK, first=True, full=1)

    @pl.loop(0, kvh + 2)
    def _(i):
        @pl.when(i < kvh)
        def _():
            drain(own_sends, i)

        @pl.when(i < kvh - 2)
        def _():
            start(own_sends, i + 2)

        @pl.when(jnp.logical_and(i < kvh, p >= 4))
        def _():
            arrived(2, i)
            start(from_l2, i)

        @pl.when(i >= kvh)
        def _():
            drain(onward, i - kvh)

        @pl.when(i >= kvh - 2)
        def _():
            start(onward, i - (kvh - 2))

        h1 = jnp.maximum(i - 1, 0)
        on1 = jnp.logical_and(jnp.logical_and(i >= 1, i <= kvh), p >= 2)

        @pl.when(on1)
        def _():
            arrived(1, h1)
            start(from_l1, h1)

        @pl.when(jnp.logical_and(i < kvh, p >= 4))
        def _():
            step(i, 0, 3, 0, BLK)
            step(i, 1, 3, BLK, BLK)

        @pl.when(on1)
        def _():
            step(h1, 0, 2, 0, BLK)
            step(h1, 1, 2, BLK, BLK)

        h0 = jnp.maximum(i - 2, 0)

        @pl.when(jnp.logical_and(i >= 2, p >= 1))
        def _():
            arrived(0, h0)
            step(h0, 0, 1, 0, 2 * BLK)
            step(h0, 1, 1, BLK, BLK)

    ssq[...] = jnp.zeros_like(ssq)

    @pl.loop(0, kvh)
    def _(h):
        for k in range(3, levels):

            @pl.when(p >= 2**k)
            def _():
                arrived(k, h)
                step(h, 0, k + 1, 0, BLK)
                step(h, 1, k + 1, BLK, BLK)

        for b in range(2):
            idx = h * 2 + b
            o = acc[idx, :, :HD] * (1.0 / acc[idx, :, HD:])
            acc[idx, :, :HD] = o
            ssq[b] += jnp.sum((o * o).reshape(group, BLK, HD), axis=0)

    swap = pltpu.make_async_remote_copy(
        src_ref=ssq, dst_ref=ssq_peer, send_sem=nsend, recv_sem=nrecv,
        device_id={"head": 1 - core}, device_id_type=MESH,
    )
    swap.start()

    for h in range(kvh):
        if h >= 2:
            drain(onward, h)
        drain(from_l2 + from_l1, h)
    swap.wait()

    def store(b, h):
        part = (pl.ds(b * BLK, BLK), pl.ds(h * group * HD, group * HD))
        return pltpu.make_async_copy(obuf.at[part], out_hbm.at[part], osem.at[b, h])

    for b in range(2):
        total = jnp.sum(ssq[b] + ssq_peer[b], axis=1, keepdims=True)
        inv = jnp.broadcast_to(lax.rsqrt(total / features + 1e-06), (BLK, HD))
        for h in range(kvh):
            for g in range(group):
                cols = slice((h * group + g) * HD, (h * group + g + 1) * HD)
                o = acc[h * 2 + b, g * BLK : (g + 1) * BLK, :HD]
                obuf[b * BLK : (b + 1) * BLK, cols] = (o * inv * gain_ref[:, cols]).astype(BF16)
            store(b, h).start()
    for b in range(2):
        for h in range(kvh):
            store(b, h).wait()


def local(queries, keyval, out_gain):
    ctx = lax.axis_size("ctx")
    levels = ctx.bit_length() - 1
    toks = queries.shape[0]
    kvh = keyval.shape[2] // HD
    heads = queries.shape[1] // HD
    group = heads // kvh
    features = queries.shape[1] * lax.axis_size("head")
    kinds = max(6, levels + 2)
    body = functools.partial(kernel, ctx, levels, kvh, group, features)
    return pl.pallas_call(
        body,
        out_shape=jax.ShapeDtypeStruct(queries.shape, BF16),
        in_specs=[
            pl.BlockSpec(memory_space=pltpu.HBM),
            pl.BlockSpec(memory_space=pltpu.HBM),
            pl.BlockSpec(memory_space=pltpu.VMEM),
        ],
        out_specs=pl.BlockSpec(memory_space=pltpu.HBM),
        scratch_shapes=[
            pltpu.VMEM((levels + 1, kvh, 2, toks, HD), BF16),
            pltpu.VMEM((heads, toks, HD), BF16),
            pltpu.VMEM((kvh * 2, group * BLK, 2 * HD), F32),
            pltpu.VMEM((kvh * 2, group * BLK, HD), F32),
            pltpu.VMEM((2, BLK, HD), F32),
            pltpu.VMEM((2, BLK, HD), F32),
            pltpu.VMEM(queries.shape, BF16),
            pltpu.SemaphoreType.DMA((heads,)),
            pltpu.SemaphoreType.DMA((kvh,)),
            pltpu.SemaphoreType.DMA((kinds, kvh)),
            pltpu.SemaphoreType.DMA((levels, kvh)),
            pltpu.SemaphoreType.DMA,
            pltpu.SemaphoreType.DMA,
            pltpu.SemaphoreType.DMA((2, kvh)),
        ],
        compiler_params=pltpu.CompilerParams(
            collective_id=0, has_side_effects=True, vmem_limit_bytes=VMEM_LIMIT
        ),
        cost_estimate=pl.CostEstimate(
            flops=2 * 2 * 2 * BLK * BLK * HD * heads * (levels + 2),
            bytes_accessed=4 * 2**20,
            transcendentals=2 * BLK * BLK * heads * (levels + 2),
        ),
    )(queries, keyval, out_gain.reshape(1, -1))


def solution(mesh):
    in_specs = (P("ctx", "head"), P(None, "ctx", "head"), P("head"))
    out_specs = P("ctx", "head")
    return jax.shard_map(local, mesh=mesh, in_specs=in_specs, out_specs=out_specs, check_vma=False)
```

```python
import functools
import math

import jax
import jax.numpy as jnp
from jax import lax
from jax.experimental import pallas as pl
from jax.experimental.pallas import tpu as pltpu
from jax.sharding import PartitionSpec as P

HD = 128
BLK = 128
MESH = pl.DeviceIdType.MESH
VMEM_LIMIT = 40 * 2**20
F32 = jnp.float32
BF16 = jnp.bfloat16


def kernel(
    ctx, levels, kvh, group, features,
    q_hbm, kv_hbm, gain_hbm, out_ref,
    kvbuf, qbuf, acc, mbuf, ssq, ssq_peer, gain,
    qsem, kvsem, send_sem, recv_sem, nsend, nrecv, gsem,
):
    p = lax.axis_index("ctx")
    core = lax.axis_index("head")
    c = HD ** (-0.5) * math.log2(math.e)
    rows = group * BLK
    bit0 = lax.rem(p, 2)
    bit1 = lax.rem(p // 2, 2)

    def kv_load(h, half):
        return pltpu.make_async_copy(
            kv_hbm.at[half, :, pl.ds(h * HD, HD)], kvbuf.at[0, h, half], kvsem.at[h, half]
        )

    def q_load(h):
        return pltpu.make_async_copy(
            q_hbm.at[:, pl.ds(h * HD, HD)], qbuf.at[h], qsem.at[h]
        )

    for h in range(kvh):
        for half in range(2):
            kv_load(h, half).start()
    for h in range(kvh * group):
        q_load(h).start()
    gain_load = pltpu.make_async_copy(gain_hbm, gain, gsem)
    gain_load.start()

    barrier = pltpu.get_barrier_semaphore()
    shifts = [1, 2, 4] + [2**k for k in range(4, levels)]
    expect = jnp.int32(1)
    pl.semaphore_signal(barrier, inc=1, device_id={"head": 1 - core}, device_id_type=MESH)
    for s in shifts:
        up = p + s < ctx
        down = p >= s

        @pl.when(up)
        def _():
            pl.semaphore_signal(barrier, inc=1, device_id={"ctx": p + s}, device_id_type=MESH)

        @pl.when(down)
        def _():
            pl.semaphore_signal(barrier, inc=1, device_id={"ctx": p - s}, device_id_type=MESH)

        expect = expect + up.astype(jnp.int32) + down.astype(jnp.int32)
    pl.semaphore_wait(barrier, expect)

    def send(src, dst, kind, h, half, target):
        return pltpu.make_async_remote_copy(
            src_ref=kvbuf.at[src, h, half],
            dst_ref=kvbuf.at[dst, h, half],
            send_sem=send_sem.at[kind, h, half],
            recv_sem=recv_sem.at[dst - 1, h, half],
            device_id={"ctx": target},
            device_id_type=MESH,
        )

    own_sends = [
        (p + 4 < ctx, 0, 3, 2, p + 4),
        (bit1 == 0, 0, 2, 1, p + 2),
        (bit0 == 0, 0, 1, 0, p + 1),
    ] + [(p + 2**k < ctx, 0, k + 1, k + 2, p + 2**k) for k in range(4, levels)]
    onward = [(jnp.logical_and(p >= 4, p + 4 < ctx), 3, 4, 4, p + 4)]
    from_l2 = [(jnp.logical_and(p >= 4, bit1 == 1), 3, 2, 3, p - 2)]
    from_l1 = [(jnp.logical_and(p >= 2, bit0 == 1), 2, 1, 5, p - 1)]

    def start(plan, h, half):
        for cond, src, dst, kind, target in plan:

            @pl.when(cond)
            def _():
                send(src, dst, kind, h, half, target).start()

    def drain(plan, h, half):
        for cond, src, dst, kind, target in plan:

            @pl.when(cond)
            def _():
                send(src, dst, kind, h, half, target).wait_send()

    def arrived(level, h, half):
        send(0, level + 1, 0, h, half, p + 1 - 2 * bit0).wait_recv()

    for h in range(kvh):
        for half in range(2):
            kv_load(h, half).wait()
            start(own_sends, h, half)

    ones = jnp.ones((2 * BLK, HD), BF16)
    lower = (
        lax.broadcasted_iota(jnp.int32, (group, BLK, BLK), 1)
        >= lax.broadcasted_iota(jnp.int32, (group, BLK, BLK), 2)
    ).reshape(rows, BLK)

    def step(h, b, slot, lo, nk, first=False, full=-1):
        idx = h * 2 + b
        q = qbuf[pl.ds(h * group, group), b * BLK : (b + 1) * BLK, :].reshape(rows, HD)
        k = kvbuf[slot, h, 0, lo : lo + nk, :]
        v = kvbuf[slot, h, 1, lo : lo + nk, :]
        s = lax.dot_general(q, k, (((1,), (1,)), ((), ())), preferred_element_type=F32)
        parts = [s[:, i : i + BLK] for i in range(0, nk, BLK)]
        parts = [x if i == full else jnp.where(lower, x, -jnp.inf) for i, x in enumerate(parts)]
        top = functools.reduce(jnp.maximum, parts)
        top = jnp.broadcast_to(jnp.max(top, axis=1, keepdims=True), (rows, BLK))
        if not first:
            old = mbuf[idx]
            top = jnp.maximum(old, top)
        w = jnp.concatenate([jnp.exp2((x - top) * c).astype(BF16) for x in parts], axis=1)
        pv = jnp.dot(
            w, jnp.concatenate([v, ones[:nk]], axis=1), preferred_element_type=F32
        )
        mbuf[idx] = top
        if first:
            acc[idx] = pv
        else:
            alpha = jnp.exp2((old - top) * c)
            acc[idx] = acc[idx] * jnp.concatenate([alpha, alpha], axis=1) + pv

    for h in range(kvh * group):
        q_load(h).wait()

    @pl.loop(0, kvh)
    def _(h):
        step(h, 0, 0, 0, BLK, first=True, full=0)
        step(h, 1, 0, 0, 2 * BLK, first=True, full=1)

    @pl.loop(0, kvh + 1)
    def _(i):
        h1 = jnp.maximum(i - 1, 0)
        on2 = jnp.logical_and(i < kvh, p >= 4)
        on1 = jnp.logical_and(i >= 1, p >= 2)
        for half in range(2):

            @pl.when(on2)
            def _():
                arrived(2, i, half)
                start(from_l2, i, half)

            @pl.when(on1)
            def _():
                arrived(1, h1, half)
                start(from_l1, h1, half)

        @pl.when(jnp.logical_and(i >= 2, i < kvh))
        def _():
            for half in range(2):
                start(onward, i - 2, half)

        @pl.when(i == kvh - 1)
        def _():
            for h in range(kvh - 2, kvh):
                for half in range(2):
                    start(onward, h, half)

        @pl.when(on2)
        def _():
            step(i, 0, 3, 0, BLK)
            step(i, 1, 3, BLK, BLK)

        @pl.when(on1)
        def _():
            step(h1, 0, 2, 0, BLK)
            step(h1, 1, 2, BLK, BLK)

    ssq[...] = jnp.zeros_like(ssq)
    gain_load.wait()

    @pl.loop(0, kvh)
    def _(h):
        @pl.when(p >= 1)
        def _():
            arrived(0, h, 0)
            arrived(0, h, 1)
            step(h, 0, 1, 0, 2 * BLK)
            step(h, 1, 1, BLK, BLK)

        for k in range(3, levels):

            @pl.when(p >= 2**k)
            def _():
                arrived(k, h, 0)
                arrived(k, h, 1)
                step(h, 0, k + 1, 0, BLK)
                step(h, 1, k + 1, BLK, BLK)

        for b in range(2):
            idx = h * 2 + b
            o = acc[idx, :, :HD] * (1.0 / acc[idx, :, HD:])
            ssq[b] += jnp.sum((o * o).reshape(group, BLK, HD), axis=0)
            for g in range(group):
                acc[idx, g * BLK : (g + 1) * BLK, :HD] = (
                    o[g * BLK : (g + 1) * BLK] * gain[pl.ds(h * group + g, 1), :]
                )

    swap = pltpu.make_async_remote_copy(
        src_ref=ssq, dst_ref=ssq_peer, send_sem=nsend, recv_sem=nrecv,
        device_id={"head": 1 - core}, device_id_type=MESH,
    )
    swap.start()

    for h in range(kvh):
        for half in range(2):
            drain(own_sends + onward + from_l2 + from_l1, h, half)
    swap.wait()

    for b in range(2):
        total = jnp.sum(ssq[b] + ssq_peer[b], axis=1, keepdims=True)
        inv = jnp.broadcast_to(lax.rsqrt(total / features + 1e-06), (BLK, HD))
        for h in range(kvh):
            for g in range(group):
                cols = slice((h * group + g) * HD, (h * group + g + 1) * HD)
                o = acc[h * 2 + b, g * BLK : (g + 1) * BLK, :HD]
                out_ref[b * BLK : (b + 1) * BLK, cols] = (o * inv).astype(BF16)


def local(queries, keyval, out_gain):
    ctx = lax.axis_size("ctx")
    levels = ctx.bit_length() - 1
    toks = queries.shape[0]
    kvh = keyval.shape[2] // HD
    heads = queries.shape[1] // HD
    group = heads // kvh
    features = queries.shape[1] * lax.axis_size("head")
    kinds = max(6, levels + 2)
    body = functools.partial(kernel, ctx, levels, kvh, group, features)
    operands = (queries, keyval, out_gain.reshape(heads, HD))
    return pl.pallas_call(
        body,
        out_shape=jax.ShapeDtypeStruct(queries.shape, BF16),
        in_specs=[
            pl.BlockSpec(memory_space=pltpu.HBM),
            pl.BlockSpec(memory_space=pltpu.HBM),
            pl.BlockSpec(memory_space=pltpu.HBM),
        ],
        out_specs=pl.BlockSpec(memory_space=pltpu.VMEM),
        scratch_shapes=[
            pltpu.VMEM((levels + 1, kvh, 2, toks, HD), BF16),
            pltpu.VMEM((heads, toks, HD), BF16),
            pltpu.VMEM((kvh * 2, group * BLK, 2 * HD), F32),
            pltpu.VMEM((kvh * 2, group * BLK, HD), F32),
            pltpu.VMEM((2, BLK, HD), F32),
            pltpu.VMEM((2, BLK, HD), F32),
            pltpu.VMEM((heads, HD), F32),
            pltpu.SemaphoreType.DMA((heads,)),
            pltpu.SemaphoreType.DMA((kvh, 2)),
            pltpu.SemaphoreType.DMA((kinds, kvh, 2)),
            pltpu.SemaphoreType.DMA((levels, kvh, 2)),
            pltpu.SemaphoreType.DMA,
            pltpu.SemaphoreType.DMA,
            pltpu.SemaphoreType.DMA,
        ],
        compiler_params=pltpu.CompilerParams(
            collective_id=0, has_side_effects=True, vmem_limit_bytes=VMEM_LIMIT
        ),
        cost_estimate=pl.CostEstimate(
            flops=2 * 2 * 2 * BLK * BLK * HD * heads * (levels + 2),
            bytes_accessed=4 * 2**20,
            transcendentals=2 * BLK * BLK * heads * (levels + 2),
        ),
    )(*(pltpu.with_memory_space_constraint(x, pltpu.HBM) for x in operands))


def solution(mesh):
    in_specs = (P("ctx", "head"), P(None, "ctx", "head"), P("head"))
    out_specs = P("ctx", "head")
    return jax.shard_map(local, mesh=mesh, in_specs=in_specs, out_specs=out_specs, check_vma=False)
```

```python
import functools
import math

import jax
import jax.numpy as jnp
from jax import lax
from jax.experimental import pallas as pl
from jax.experimental.pallas import tpu as pltpu
from jax.sharding import PartitionSpec as P

HD = 128
BLK = 128
MESH = pl.DeviceIdType.MESH
VMEM_LIMIT = 40 * 2**20
F32 = jnp.float32
BF16 = jnp.bfloat16


def kernel(
    ctx, levels, kvh, group, features,
    q_hbm, kv_hbm, gain_hbm, out_ref,
    kvbuf, qbuf, acc, mbuf, ssq, ssq_peer, gain,
    qsem, kvsem, send_sem, recv_sem, nsend, nrecv, gsem,
):
    p = lax.axis_index("ctx")
    core = lax.axis_index("head")
    c = HD ** (-0.5) * math.log2(math.e)
    rows = group * BLK
    bit0 = lax.rem(p, 2)
    bit1 = lax.rem(p // 2, 2)

    def kv_load(h, half):
        return pltpu.make_async_copy(
            kv_hbm.at[half, :, pl.ds(h * HD, HD)], kvbuf.at[0, h, half], kvsem.at[h, half]
        )

    def q_load(h):
        return pltpu.make_async_copy(
            q_hbm.at[:, pl.ds(h * HD, HD)], qbuf.at[h], qsem.at[h]
        )

    for h in range(kvh):
        for half in range(2):
            kv_load(h, half).start()
    for h in range(kvh * group):
        q_load(h).start()
    gain_load = pltpu.make_async_copy(gain_hbm, gain, gsem)
    gain_load.start()

    barrier = pltpu.get_barrier_semaphore()
    shifts = [1, 2, 4] + [2**k for k in range(4, levels)]
    expect = jnp.int32(1)
    pl.semaphore_signal(barrier, inc=1, device_id={"head": 1 - core}, device_id_type=MESH)
    for s in shifts:
        up = p + s < ctx
        down = p >= s

        @pl.when(up)
        def _():
            pl.semaphore_signal(barrier, inc=1, device_id={"ctx": p + s}, device_id_type=MESH)

        @pl.when(down)
        def _():
            pl.semaphore_signal(barrier, inc=1, device_id={"ctx": p - s}, device_id_type=MESH)

        expect = expect + up.astype(jnp.int32) + down.astype(jnp.int32)
    pl.semaphore_wait(barrier, expect)

    def send(src, dst, kind, h, half, target):
        return pltpu.make_async_remote_copy(
            src_ref=kvbuf.at[src, h, half],
            dst_ref=kvbuf.at[dst, h, half],
            send_sem=send_sem.at[kind, h, half],
            recv_sem=recv_sem.at[dst - 1, h, half],
            device_id={"ctx": target},
            device_id_type=MESH,
        )

    own_sends = [
        (p + 4 < ctx, 0, 3, 2, p + 4),
        (bit1 == 0, 0, 2, 1, p + 2),
        (bit0 == 0, 0, 1, 0, p + 1),
    ] + [(p + 2**k < ctx, 0, k + 1, k + 2, p + 2**k) for k in range(4, levels)]
    onward = [(jnp.logical_and(p >= 4, p + 4 < ctx), 3, 4, 4, p + 4)]
    from_l2 = [(jnp.logical_and(p >= 4, bit1 == 1), 3, 2, 3, p - 2)]
    from_l1 = [(jnp.logical_and(p >= 2, bit0 == 1), 2, 1, 5, p - 1)]

    def start(plan, h, half):
        for cond, src, dst, kind, target in plan:

            @pl.when(cond)
            def _():
                send(src, dst, kind, h, half, target).start()

    def drain(plan, h, half):
        for cond, src, dst, kind, target in plan:

            @pl.when(cond)
            def _():
                send(src, dst, kind, h, half, target).wait_send()

    def arrived(level, h, half):
        send(0, level + 1, 0, h, half, p + 1 - 2 * bit0).wait_recv()

    for h in range(kvh):
        for half in range(2):
            kv_load(h, half).wait()
            start(own_sends, h, half)

    ones = jnp.ones((2 * BLK, HD), BF16)
    lower = (
        lax.broadcasted_iota(jnp.int32, (group, BLK, BLK), 1)
        >= lax.broadcasted_iota(jnp.int32, (group, BLK, BLK), 2)
    ).reshape(rows, BLK)

    def scored(h, b, slot, lo, nk, first=False, full=-1):
        idx = h * 2 + b
        q = qbuf[pl.ds(h * group, group), b * BLK : (b + 1) * BLK, :].reshape(rows, HD)
        k = kvbuf[slot, h, 0, lo : lo + nk, :]
        s = lax.dot_general(q, k, (((1,), (1,)), ((), ())), preferred_element_type=F32)
        parts = [s[:, i : i + BLK] for i in range(0, nk, BLK)]
        parts = [x if i == full else jnp.where(lower, x, -jnp.inf) for i, x in enumerate(parts)]
        top = functools.reduce(jnp.maximum, parts)
        top = jnp.broadcast_to(jnp.max(top, axis=1, keepdims=True), (rows, BLK))
        if not first:
            old = mbuf[idx]
            top = jnp.maximum(old, top)
        w = jnp.concatenate([jnp.exp2((x - top) * c).astype(BF16) for x in parts], axis=1)
        mbuf[idx] = top
        alpha = None if first else jnp.exp2((old - top) * c)

        def finish():
            v = kvbuf[slot, h, 1, lo : lo + nk, :]
            pv = jnp.dot(
                w, jnp.concatenate([v, ones[:nk]], axis=1), preferred_element_type=F32
            )
            if first:
                acc[idx] = pv
            else:
                acc[idx] = acc[idx] * jnp.concatenate([alpha, alpha], axis=1) + pv

        return finish

    def step(*args, **options):
        scored(*args, **options)()

    for h in range(kvh * group):
        q_load(h).wait()

    @pl.loop(0, kvh)
    def _(h):
        step(h, 0, 0, 0, BLK, first=True, full=0)
        step(h, 1, 0, 0, 2 * BLK, first=True, full=1)

    @pl.loop(0, kvh + 1)
    def _(i):
        h1 = jnp.maximum(i - 1, 0)
        on2 = jnp.logical_and(i < kvh, p >= 4)
        on1 = jnp.logical_and(i >= 1, p >= 2)
        for half in range(2):

            @pl.when(on2)
            def _():
                arrived(2, i, half)
                start(from_l2, i, half)

            @pl.when(on1)
            def _():
                arrived(1, h1, half)
                start(from_l1, h1, half)

        @pl.when(jnp.logical_and(i >= 2, i < kvh))
        def _():
            for half in range(2):
                start(onward, i - 2, half)

        @pl.when(i == kvh - 1)
        def _():
            for h in range(kvh - 2, kvh):
                for half in range(2):
                    start(onward, h, half)

        @pl.when(on2)
        def _():
            step(i, 0, 3, 0, BLK)
            step(i, 1, 3, BLK, BLK)

        @pl.when(on1)
        def _():
            step(h1, 0, 2, 0, BLK)
            step(h1, 1, 2, BLK, BLK)

    ssq[...] = jnp.zeros_like(ssq)
    gain_load.wait()

    @pl.loop(0, kvh)
    def _(h):
        @pl.when(p >= 1)
        def _():
            arrived(0, h, 0)
            arrived(0, h, 1)
            step(h, 0, 1, 0, 2 * BLK)
            step(h, 1, 1, BLK, BLK)

        for k in range(3, levels):

            @pl.when(p >= 2**k)
            def _():
                arrived(k, h, 0)
                finish = [scored(h, b, k + 1, b * BLK, BLK) for b in range(2)]
                arrived(k, h, 1)
                for rest in finish:
                    rest()

        for b in range(2):
            idx = h * 2 + b
            o = acc[idx, :, :HD] * (1.0 / acc[idx, :, HD:])
            ssq[b] += jnp.sum((o * o).reshape(group, BLK, HD), axis=0)
            for g in range(group):
                acc[idx, g * BLK : (g + 1) * BLK, :HD] = (
                    o[g * BLK : (g + 1) * BLK] * gain[pl.ds(h * group + g, 1), :]
                )

    swap = pltpu.make_async_remote_copy(
        src_ref=ssq, dst_ref=ssq_peer, send_sem=nsend, recv_sem=nrecv,
        device_id={"head": 1 - core}, device_id_type=MESH,
    )
    swap.start()

    for h in range(kvh):
        for half in range(2):
            drain(own_sends + onward + from_l2 + from_l1, h, half)
    swap.wait()

    for b in range(2):
        total = jnp.sum(ssq[b] + ssq_peer[b], axis=1, keepdims=True)
        inv = jnp.broadcast_to(lax.rsqrt(total / features + 1e-06), (BLK, HD))
        for h in range(kvh):
            for g in range(group):
                cols = slice((h * group + g) * HD, (h * group + g + 1) * HD)
                o = acc[h * 2 + b, g * BLK : (g + 1) * BLK, :HD]
                out_ref[b * BLK : (b + 1) * BLK, cols] = (o * inv).astype(BF16)


def local(queries, keyval, out_gain):
    ctx = lax.axis_size("ctx")
    levels = ctx.bit_length() - 1
    toks = queries.shape[0]
    kvh = keyval.shape[2] // HD
    heads = queries.shape[1] // HD
    group = heads // kvh
    features = queries.shape[1] * lax.axis_size("head")
    kinds = max(6, levels + 2)
    body = functools.partial(kernel, ctx, levels, kvh, group, features)
    operands = (queries, keyval, out_gain.reshape(heads, HD))
    return pl.pallas_call(
        body,
        out_shape=jax.ShapeDtypeStruct(queries.shape, BF16),
        in_specs=[
            pl.BlockSpec(memory_space=pltpu.HBM),
            pl.BlockSpec(memory_space=pltpu.HBM),
            pl.BlockSpec(memory_space=pltpu.HBM),
        ],
        out_specs=pl.BlockSpec(memory_space=pltpu.VMEM),
        scratch_shapes=[
            pltpu.VMEM((levels + 1, kvh, 2, toks, HD), BF16),
            pltpu.VMEM((heads, toks, HD), BF16),
            pltpu.VMEM((kvh * 2, group * BLK, 2 * HD), F32),
            pltpu.VMEM((kvh * 2, group * BLK, HD), F32),
            pltpu.VMEM((2, BLK, HD), F32),
            pltpu.VMEM((2, BLK, HD), F32),
            pltpu.VMEM((heads, HD), F32),
            pltpu.SemaphoreType.DMA((heads,)),
            pltpu.SemaphoreType.DMA((kvh, 2)),
            pltpu.SemaphoreType.DMA((kinds, kvh, 2)),
            pltpu.SemaphoreType.DMA((levels, kvh, 2)),
            pltpu.SemaphoreType.DMA,
            pltpu.SemaphoreType.DMA,
            pltpu.SemaphoreType.DMA,
        ],
        compiler_params=pltpu.CompilerParams(
            collective_id=0, has_side_effects=True, vmem_limit_bytes=VMEM_LIMIT
        ),
        cost_estimate=pl.CostEstimate(
            flops=2 * 2 * 2 * BLK * BLK * HD * heads * (levels + 2),
            bytes_accessed=4 * 2**20,
            transcendentals=2 * BLK * BLK * heads * (levels + 2),
        ),
    )(*(pltpu.with_memory_space_constraint(x, pltpu.HBM) for x in operands))


def solution(mesh):
    in_specs = (P("ctx", "head"), P(None, "ctx", "head"), P("head"))
    out_specs = P("ctx", "head")
    return jax.shard_map(local, mesh=mesh, in_specs=in_specs, out_specs=out_specs, check_vma=False)
```
